32 devices in a mesh: groups: 2 (over x), slab: 16 (over z, y, core).
Axes of the slice: x: 2, y: 2, z: 4, core: 2. Of those that a mesh axis runs over, the one named last changes fastest.
Arguments:
- atomic_descriptors: float32 [98304, 128], P(('groups', 'slab')), parts along dimension 0, may hold values from -80 to 80
- fractional_locations: float32 [3, 98304], P(None, ('groups', 'slab')), parts along dimension 1, may hold values from 0 to 1
- filled_slot_tallies: int32 [32], P(('groups', 'slab')), parts along dimension 0, may hold values from 0 to 3072, as said below
- reciprocal_lattice_indices: int32 [3, 1024], replicated, may hold values from -8 to 8
- spectral_kernels: float32 [2, 1024, 128], replicated, may hold values from -0.1875 to 0.1875
- initial_mixing_matrix: float32 [2, 128, 128], replicated, may hold values from -0.5 to 0.5
- closing_mixing_matrix: float32 [2, 128, 128], replicated, may hold values from -0.5 to 0.5
Outputs:
- features_out: float32 [98304, 128], P(('groups', 'slab')), parts along dimension 0
The draws below stay inside these ranges and needn't reach their ends.
There are 2 independent parts, one for each index of `groups`. The reference program is written for one: setup_inputs(seed, part) draws one part's arguments, and reference() takes and returns one part's arrays. A program takes and returns all parts, laid end to end along the dimension named above; an argument that names none is the same for every part. Nothing has to cross between parts.
Inputs may be any that keep to these rules, and one draw needn't show every extreme that they name: Write b(i) for filled_slot_tallies[i] / 128 rounded up. For every i < 8: b(i) + b(i + 8) <= 24, with equality for i = 7.
All inputs are finite; a program needn't handle non-finite values.
Results may differ from the reference program's by a relative error of at most 0.0003.
Values sent between devices are 32-bit elements; how exact they have to be, the bound alone decides.
A program may use at most 64 MiB of HBM per device.

```python
import math
import jax
import jax.numpy as jnp
from jax import lax

C = 128
KSPACE_TOTAL = 1024
BLK = 128
WORKB = 12
CAP = 3072
SLOTS = 49152
N_SLAB = 16


def draw_filled_slot_tallies(key, part):
    key = jax.random.fold_in(key, 11)
    pairs = N_SLAB // 2
    rank = jnp.arange(pairs, dtype=jnp.int32)
    key_drop, key_light, key_heavy_fill, key_light_fill, key_side = jax.random.split(key, 5)
    ceiling = WORKB + 1 + (WORKB - 1) * (rank + 1) // pairs
    lowered = jax.random.randint(key_drop, (pairs,), 0, 2)
    heavy = jnp.maximum(ceiling - jnp.where(rank == pairs - 1, 0, lowered), WORKB + 1)
    light = jax.random.randint(key_light, (pairs,), 0, 2 * WORKB - heavy + 1)
    heavy_fill = jax.random.randint(key_heavy_fill, (pairs,), BLK // 2, BLK + 1)
    heavy_fill = jnp.where(rank == pairs - 1, BLK, heavy_fill)
    light_fill = jax.random.randint(key_light_fill, (pairs,), 1, BLK + 1)
    heavy_atoms = (heavy - 1) * BLK + heavy_fill
    light_atoms = jnp.where(light > 0, (light - 1) * BLK + light_fill, 0)
    heavy_low = jax.random.randint(key_side, (pairs,), 0, 2)
    heavy_low = jnp.where(rank == 0, jnp.asarray(part, jnp.int32) % 2, heavy_low)
    heavy_low = jnp.where(rank == pairs - 1, (jnp.asarray(part, jnp.int32) + 1) % 2, heavy_low)
    lower_side = jnp.where(heavy_low == 1, heavy_atoms, light_atoms)
    upper_side = jnp.where(heavy_low == 1, light_atoms, heavy_atoms)
    return jnp.concatenate([lower_side, upper_side]).astype(jnp.int32)


def draw_fractional_locations(key, part):
    key = jax.random.fold_in(key, 37)
    key_side, key_depth = jax.random.split(key, 2)
    lateral = jax.random.uniform(key_side, (2, SLOTS), jnp.float32)
    along = jax.random.uniform(key_depth, (1, SLOTS), jnp.float32)
    layer_index = (jnp.arange(SLOTS, dtype=jnp.int32) // CAP).astype(jnp.float32)
    depth = (layer_index[None, :] + along) / N_SLAB
    return jnp.concatenate([lateral, depth], axis=0).astype(jnp.float32)


def draw_atomic_descriptors(key, part):
    key = jax.random.fold_in(key, 23)
    key_atom, key_chan, key_offset, key_tilt, noise_key_split = jax.random.split(key, 5)
    depth = (jnp.arange(SLOTS, dtype=jnp.int32) // CAP).astype(jnp.float32) / N_SLAB
    atom_scale = jnp.exp(jax.random.uniform(key_atom, (SLOTS, 1), jnp.float32, math.log(0.3), math.log(3.0)))
    chan_scale = jnp.exp(jax.random.uniform(key_chan, (1, C), jnp.float32, math.log(0.5), math.log(2.0)))
    offset = jax.random.uniform(key_offset, (1, C), jnp.float32, -1.0, 1.0)
    tilt = jax.random.uniform(key_tilt, (1, C), jnp.float32, -1.0, 1.0)
    noise = jnp.clip(jax.random.normal(noise_key_split, (SLOTS, C), jnp.float32), -5.0, 5.0)
    values = atom_scale * chan_scale * (offset + tilt * (2.0 * depth[:, None] - 1.0) + noise)
    return values.astype(jnp.float32)


def plant(result, own_key, least, high):
    shape = result.shape
    spot = [jax.random.randint(jax.random.fold_in(own_key, axis), (), 0, shape[axis]) for axis in range(len(shape))]
    result = result.at[tuple(spot)].set(least)
    longest = shape.index(max(shape))
    spot[longest] = (spot[longest] + 1) % shape[longest]
    return result.at[tuple(spot)].set(high)


def centred(key, shape, scale, bound, kind=jnp.bfloat16):
    entries = scale * jax.random.normal(key, shape, jnp.float32)
    return jnp.clip(entries, min=-bound, max=bound).astype(kind)


def setup_inputs(seed: int = 0, part: int = 0) -> dict:
    splits = jax.random.split(jax.random.key(seed), 8)
    part_splits = jax.random.split(jax.random.fold_in(splits[7], part), 8)
    atomic_descriptors = draw_atomic_descriptors(jax.random.fold_in(jax.random.fold_in(splits[7], part), 71), part)
    fractional_locations = draw_fractional_locations(jax.random.fold_in(jax.random.fold_in(splits[7], part), 71), part)
    filled_slot_tallies = draw_filled_slot_tallies(jax.random.fold_in(jax.random.fold_in(splits[7], part), 71), part)
    reciprocal_lattice_indices = plant(jax.random.randint(splits[3], (3, KSPACE_TOTAL), -8, 9), jax.random.fold_in(splits[3], 1), -8, 8).astype(jnp.int32)
    spectral_kernels = centred(splits[4], (2, KSPACE_TOTAL, C), KSPACE_TOTAL ** -0.5, 0.1875, jnp.float32)
    initial_mixing_matrix = centred(splits[5], (2, C, C), C ** -0.5, 0.5, jnp.float32)
    closing_mixing_matrix = centred(splits[6], (2, C, C), C ** -0.5, 0.5, jnp.float32)
    return {"atomic_descriptors": atomic_descriptors, "fractional_locations": fractional_locations, "filled_slot_tallies": filled_slot_tallies, "reciprocal_lattice_indices": reciprocal_lattice_indices, "spectral_kernels": spectral_kernels, "initial_mixing_matrix": initial_mixing_matrix, "closing_mixing_matrix": closing_mixing_matrix}


HIGHEST_PREC = lax.Precision.HIGHEST
TWO_PI = 2.0 * math.pi

def phase_rows(coords, reciprocal_momenta):
    theta = TWO_PI * (coords[0][:, None] * reciprocal_momenta[0][None, :] + coords[1][:, None] * reciprocal_momenta[1][None, :] + coords[2][:, None] * reciprocal_momenta[2][None, :])
    return jnp.concatenate([jnp.cos(theta), jnp.sin(theta)], axis=1)

def refine(states, potential_rows, first_matrix, second_matrix):
    inner = jax.nn.silu(jnp.dot(potential_rows, first_matrix, precision=HIGHEST_PREC))
    return states + jnp.dot(inner, second_matrix, precision=HIGHEST_PREC)

def factor_weights(s_raw, density, charge, total, stacked):
    mean_charge = charge / total
    return (s_raw - density[:, None] * mean_charge[None, :]) / jnp.sqrt(total) * stacked

def reference(atomic_descriptors, fractional_locations, filled_slot_tallies, reciprocal_lattice_indices, spectral_kernels, initial_mixing_matrix, closing_mixing_matrix):
    slabs = filled_slot_tallies.shape[0]
    slots = atomic_descriptors.shape[0] // slabs
    channels = atomic_descriptors.shape[1]
    reciprocal_momenta = reciprocal_lattice_indices.astype(jnp.float32)
    width = 2 * reciprocal_momenta.shape[1]
    occupied = (jnp.arange(slots, dtype=jnp.int32)[None, :] < filled_slot_tallies[:, None]).astype(jnp.float32)
    states = atomic_descriptors.reshape(slabs, slots, channels)
    coords = jnp.moveaxis(fractional_locations.reshape(3, slabs, slots), 1, 0)
    total = jnp.sum(filled_slot_tallies).astype(jnp.float32)
    for layer in range(2):

        def accumulate(running, block_item):
            states_now, coords_now, occupied_now = block_item
            phases = phase_rows(coords_now, reciprocal_momenta)
            weighted = states_now * occupied_now[:, None]
            return ((running[0] + jnp.dot(phases.T, weighted, precision=HIGHEST_PREC), running[1] + jnp.dot(occupied_now, phases, precision=HIGHEST_PREC), running[2] + lax.optimization_barrier(jnp.sum(weighted, axis=0))), None)
        start_sums = (jnp.zeros((width, channels), jnp.float32), jnp.zeros((width,), jnp.float32), jnp.zeros((channels,), jnp.float32))
        (s_raw, density, charge), _ = lax.scan(accumulate, start_sums, (states, coords, occupied))
        stacked = jnp.concatenate([spectral_kernels[layer], spectral_kernels[layer]], axis=0)
        weights = factor_weights(s_raw, density, charge, total, stacked)

        def advance(block_item):
            states_now, coords_now = block_item
            potential_rows = jnp.dot(phase_rows(coords_now, reciprocal_momenta), weights, precision=HIGHEST_PREC)
            return refine(states_now, potential_rows, initial_mixing_matrix[layer], closing_mixing_matrix[layer])
        states = lax.map(advance, (states, coords))
    return (states * occupied[:, :, None]).reshape(slabs * slots, channels)
```

```python
import functools
import math

import jax
import jax.numpy as jnp
from jax import lax
from jax.experimental import pallas as pl
from jax.experimental.pallas import tpu as pltpu
from jax.sharding import PartitionSpec as P
import numpy as np

TILE = 256
HALF_TURN_SPAN = 0.5


def fit_half_angle():
    nodes = np.cos((np.arange(400) + 0.5) * np.pi / 400) * HALF_TURN_SPAN
    square = nodes * nodes
    root = math.sqrt(2.0)
    odd = np.stack([nodes * square**i for i in range(5)], 1)
    even = np.stack([square**i for i in range(5)], 1)
    sin_fit = np.linalg.lstsq(odd, root * np.sin(np.pi * nodes), rcond=None)[0]
    cos_fit = np.linalg.lstsq(even, root * np.cos(np.pi * nodes), rcond=None)[0]
    return [float(v) for v in sin_fit], [float(v) for v in cos_fit]


SIN_FIT, COS_FIT = fit_half_angle()


def horner(square, coefs):
    value = coefs[-1] * square + coefs[-2]
    for coef in coefs[-3::-1]:
        value = value * square + coef
    return value


def split(value):
    high = value.astype(jnp.bfloat16)
    return high, (value - high.astype(jnp.float32)).astype(jnp.bfloat16)


def cos_sin_turns(turns):
    magic = 12582912.0
    rest = turns - ((turns + magic) - magic)
    square = rest * rest
    s = rest * horner(square, SIN_FIT)
    c = horner(square, COS_FIT)
    return 1.0 - s * s, s * c


def dot(a, b, dims):
    return lax.dot_general(a, b, (dims, ((), ())), preferred_element_type=jnp.float32)


def dot_hp(a, b):
    return lax.dot_general(
        a, b, (((1,), (0,)), ((), ())),
        precision=lax.Precision.HIGHEST, preferred_element_type=jnp.float32,
    )


NN = ((1,), (0,))
NT = ((1,), (1,))
TN = ((0,), (0,))


def occupied_row(tally, first, width):
    return (first + lax.broadcasted_iota(jnp.int32, (1, width), 1) < tally).astype(jnp.float32)


def coordinate_parts(coords):
    high = coords.astype(jnp.bfloat16).astype(jnp.float32)
    rest = coords - high
    mid = rest.astype(jnp.bfloat16).astype(jnp.float32)
    low = rest - mid
    return jnp.concatenate([high, mid, low, jnp.zeros_like(low)], axis=0).astype(jnp.bfloat16)


def update(states_t, high, low, w_high, w_low, first_t, second_t):
    c = w_high.shape[0]
    both = dot(jnp.concatenate([w_high, w_low], 0), high, NT)
    potential = both[:c] + both[c:] + dot(w_high, low, NT)
    v = dot_hp(first_t, potential)
    return states_t + dot_hp(second_t, v / (1.0 + jnp.exp(-v)))


def first_kernel(tally, states, coords, k_parts, high_out, low_out, s_out, density_out, charge_out):
    i = pl.program_id(0)
    kspace = k_parts.shape[1]
    c = states.shape[1]
    occ = occupied_row(tally[0], i * TILE, TILE)
    weighted = states[...].T * occ
    w_high, w_low = split(weighted)
    occ16 = jnp.broadcast_to(occ, (16, TILE)).astype(jnp.bfloat16)
    lhs_high = jnp.concatenate([w_high, w_low, occ16], 0)
    lhs_low = jnp.concatenate([w_high, occ16], 0)
    parts = coordinate_parts(coords[...])

    @pl.when(i == 0)
    def _():
        s_out[...] = jnp.zeros_like(s_out)
        density_out[...] = jnp.zeros_like(density_out)
        charge_out[...] = jnp.zeros_like(charge_out)

    charge_out[...] += jnp.broadcast_to(jnp.sum(weighted, axis=1, keepdims=True), charge_out.shape)
    step = 256
    for k in range(0, kspace, step):
        turns = dot(parts, k_parts[:, k : k + step], TN)
        for value, at in zip(cos_sin_turns(turns), (k, kspace + k)):
            high, low = split(value)
            high_out[:, at : at + step] = high
            low_out[:, at : at + step] = low
            one = dot(lhs_high, high, NN)
            two = dot(lhs_low, low, NN)
            s_out[:, at : at + step] += one[:c] + one[c : 2 * c] + two[:c]
            density_out[:, at : at + step] += (one[2 * c :] + two[c:])[:8]


def middle_kernel(tally, states, high, low, w_high, w_low, first_t, second_t, fresh_out, s_out, charge_out):
    i = pl.program_id(0)
    c = states.shape[1]
    occ = occupied_row(tally[0], i * TILE, TILE)

    @pl.when(i == 0)
    def _():
        s_out[...] = jnp.zeros_like(s_out)
        charge_out[...] = jnp.zeros_like(charge_out)

    fresh = update(
        states[...].T, high[...], low[...], w_high[...], w_low[...], first_t[...], second_t[...]
    )
    fresh_out[...] = fresh
    weighted = fresh * occ
    charge_out[...] += jnp.broadcast_to(jnp.sum(weighted, axis=1, keepdims=True), charge_out.shape)
    x_high, x_low = split(weighted)
    one = dot(jnp.concatenate([x_high, x_low], 0), high[...], NN)
    s_out[...] += one[:c] + one[c:] + dot(x_high, low[...], NN)


def last_kernel(tally, states_t, high, low, w_high, w_low, first_t, second_t, out):
    i = pl.program_id(0)
    occ = occupied_row(tally[0], i * TILE, TILE)
    fresh = update(
        states_t[...], high[...], low[...], w_high[...], w_low[...], first_t[...], second_t[...]
    )
    out[...] = (fresh * occ).T


def body(states, coords, tallies, lattice, kernels, first_matrix, second_matrix):
    slots, c = states.shape
    kspace = lattice.shape[1]
    width = 2 * kspace
    grid = (slots // TILE,)
    f32, b16 = jnp.float32, jnp.bfloat16
    shape = jax.ShapeDtypeStruct
    coords8 = jnp.pad(coords, ((0, 5), (0, 0)))
    k8 = jnp.pad(lattice, ((0, 5), (0, 0))).astype(b16)
    k_parts = jnp.concatenate([k8, k8, k8, k8], 0)
    first_t = jnp.swapaxes(first_matrix, 1, 2)
    second_t = jnp.swapaxes(second_matrix, 1, 2)
    kernels_t = jnp.swapaxes(kernels, 1, 2)

    tally_spec = pl.BlockSpec(memory_space=pltpu.SMEM)
    rows = lambda n: pl.BlockSpec((TILE, n), lambda i: (i, 0))
    lanes = lambda n: pl.BlockSpec((n, TILE), lambda i: (0, i))
    whole = lambda *s: pl.BlockSpec(s, lambda i: (0,) * len(s))
    params = pltpu.CompilerParams(vmem_limit_bytes=60 * 2**20)

    high, low, s, density, charge = pl.pallas_call(
        first_kernel,
        grid=grid,
        in_specs=[tally_spec, rows(c), lanes(8), whole(32, kspace)],
        out_specs=[rows(width), rows(width), whole(c, width), whole(8, width), whole(c, 128)],
        out_shape=[
            shape((slots, width), b16), shape((slots, width), b16),
            shape((c, width), f32), shape((8, width), f32), shape((c, 128), f32),
        ],
        compiler_params=params,
    )(tallies, states, coords8, k_parts)

    total = tallies[0].astype(f32)
    s, density, charge, total = lax.psum((s, density[:1], charge[:, :1], total), "slab")

    def weights(s, charge, kernel_t):
        w = (s - (charge / total) * density) / jnp.sqrt(total) * jnp.concatenate([kernel_t, kernel_t], 1)
        w_high = lax.reduce_precision(w, 8, 7)
        return w_high.astype(b16), (w - w_high).astype(b16)

    w_high, w_low = weights(s, charge, kernels_t[0])
    common = [rows(width), rows(width), whole(c, width), whole(c, width), whole(c, c), whole(c, c)]
    fresh, s, charge = pl.pallas_call(
        middle_kernel,
        grid=grid,
        in_specs=[tally_spec, rows(c)] + common,
        out_specs=[lanes(c), whole(c, width), whole(c, 128)],
        out_shape=[shape((c, slots), f32), shape((c, width), f32), shape((c, 128), f32)],
        compiler_params=params,
    )(tallies, states, high, low, w_high, w_low, first_t[0], second_t[0])
    s, charge = lax.psum((s, charge[:, :1]), "slab")
    w_high, w_low = weights(s, charge, kernels_t[1])
    return pl.pallas_call(
        last_kernel,
        grid=grid,
        in_specs=[tally_spec, lanes(c)] + common,
        out_specs=rows(c),
        out_shape=shape((slots, c), f32),
        compiler_params=params,
    )(tallies, fresh, high, low, w_high, w_low, first_t[1], second_t[1])


def solution(mesh):
    in_specs = (
        P(("groups", "slab"), None),
        P(None, ("groups", "slab")),
        P(("groups", "slab")),
        P(),
        P(),
        P(),
        P(),
    )
    out_specs = P(("groups", "slab"), None)
    return jax.shard_map(body, mesh=mesh, in_specs=in_specs, out_specs=out_specs, check_vma=False)
```

```python
import functools
import math

import jax
import jax.numpy as jnp
from jax import lax
from jax.experimental import pallas as pl
from jax.experimental.pallas import tpu as pltpu
from jax.sharding import PartitionSpec as P
import numpy as np

TILE = 512
PIECES = 3
HALF_TURN_SPAN = 0.5


def fit_half_angle():
    nodes = np.cos((np.arange(400) + 0.5) * np.pi / 400) * HALF_TURN_SPAN
    square = nodes * nodes
    root = math.sqrt(2.0)
    odd = np.stack([nodes * square**i for i in range(5)], 1)
    even = np.stack([square**i for i in range(5)], 1)
    sin_fit = np.linalg.lstsq(odd, root * np.sin(np.pi * nodes), rcond=None)[0]
    cos_fit = np.linalg.lstsq(even, root * np.cos(np.pi * nodes), rcond=None)[0]
    return [float(v) for v in sin_fit], [float(v) for v in cos_fit]


SIN_FIT, COS_FIT = fit_half_angle()


def horner(square, coefs):
    value = coefs[-1] * square + coefs[-2]
    for coef in coefs[-3::-1]:
        value = value * square + coef
    return value


def split(value):
    high = value.astype(jnp.bfloat16)
    return high, (value - high.astype(jnp.float32)).astype(jnp.bfloat16)


def cos_sin_turns(turns):
    magic = 12582912.0
    rest = turns - ((turns + magic) - magic)
    square = rest * rest
    s = rest * horner(square, SIN_FIT)
    c = horner(square, COS_FIT)
    return 1.0 - s * s, s * c


def dot(a, b, dims):
    return lax.dot_general(a, b, (dims, ((), ())), preferred_element_type=jnp.float32)


NN = ((1,), (0,))
TN = ((0,), (0,))


def coordinate_parts(coords):
    high = coords.astype(jnp.bfloat16).astype(jnp.float32)
    rest = coords - high
    mid = rest.astype(jnp.bfloat16).astype(jnp.float32)
    low = rest - mid
    return jnp.concatenate([high, mid, low, jnp.zeros_like(low)], axis=0).astype(jnp.bfloat16)


MESH = pl.DeviceIdType.MESH


def run_tiles(lo, hi, step, body_at):
    def trip(t, _):
        body_at(pl.multiple_of(t * step, step))
        return 0

    lax.fori_loop(lo // step, hi // step, trip, 0)


def partner_of(me, bit):
    b = lax.rem(lax.div(me, 1 << bit), 2)
    return b, me + (1 - 2 * b) * (1 << bit)


def sum_steps(me, order, part, full, recv, send_sems, recv_sems):
    lo, n, at, sem = 0, part.shape[0], 0, 0
    for bit in order:
        b, other = partner_of(me, bit)
        half = n // 2
        gone = pl.multiple_of(lo + (1 - b) * half, 8)
        kept = pl.multiple_of(lo + b * half, 8)
        copy = pltpu.make_async_remote_copy(
            part.at[pl.ds(gone, half)], recv.at[pl.ds(at, half)],
            send_sems.at[sem], recv_sems.at[sem],
            device_id={"slab": other}, device_id_type=MESH,
        )
        copy.start()
        yield
        copy.wait()
        part[pl.ds(kept, half), :] += recv[at : at + half, :]
        lo, n, at, sem = kept, half, at + half, sem + 1
    full[pl.ds(lo, n), :] = part[pl.ds(lo, n), :]
    for bit in order[::-1]:
        b, other = partner_of(me, bit)
        rows = pl.ds(pl.multiple_of(lo, 8), n)
        copy = pltpu.make_async_remote_copy(
            full.at[rows], full.at[rows],
            send_sems.at[sem], recv_sems.at[sem],
            device_id={"slab": other}, device_id_type=MESH,
        )
        copy.start()
        yield
        copy.wait()
        lo, n, sem = lo - b * n, n * 2, sem + 1


def small_steps(me, bits, part, recv, send_sems, recv_sems):
    for bit in range(bits):
        _, other = partner_of(me, bit)
        copy = pltpu.make_async_remote_copy(
            part.at[bit], recv.at[bit], send_sems.at[bit], recv_sems.at[bit],
            device_id={"slab": other}, device_id_type=MESH,
        )
        copy.start()
        yield
        copy.wait()
        part[bit + 1] = part[bit] + recv[bit]


def advance(*steps):
    live = False
    for one in steps:
        live = next(one, "end") != "end" or live
    return live


def times_split(a, matrix):
    c = matrix.shape[1]
    m_high, m_low = split(matrix)
    a_high, a_low = split(a)
    both = dot(a_high, jnp.concatenate([m_high, m_low], 1), NN)
    return both[:, :c] + both[:, c:] + dot(a_low, m_high, NN)


def ewald_kernel(
    bits, tally, states, coords, k_parts, kernels, first_matrix, second_matrix, out,
    high, low, lhs, sums, density, charge, w, fresh, potential,
    part, full, recv, small, small_recv, s_send, s_recv, x_send, x_recv,
):
    me = lax.axis_index("slab")
    slots, c = states.shape
    kh = part.shape[2] // 2
    wide = 2 * kh

    barrier = pltpu.get_barrier_semaphore()
    for bit in range(bits):
        pl.semaphore_signal(barrier, inc=1, device_id={"slab": partner_of(me, bit)[1]}, device_id_type=MESH)
    pl.semaphore_wait(barrier, bits)

    orders = [list(range(bits)), [0] + list(range(2, bits)) + [1]]

    def big(layer, half):
        return sum_steps(
            me, orders[half], part.at[layer, half], full.at[layer, half], recv.at[layer, half],
            s_send.at[layer, half], s_recv.at[layer, half],
        )

    def little(layer):
        return small_steps(me, bits, small.at[layer], small_recv.at[layer], x_send.at[layer], x_recv.at[layer])

    def occ_column(at):
        rows = at + lax.broadcasted_iota(jnp.int32, (TILE, c), 0)
        return (rows < tally[0]).astype(jnp.float32)

    def place_lhs(at, masked):
        flipped = masked.T
        x_high, x_low = split(flipped)
        lhs[:c, pl.ds(at, TILE)] = x_high
        lhs[c : 2 * c, pl.ds(at, TILE)] = x_low

    def phases(half, at):
        columns = coordinate_parts(coords[:, pl.ds(at, TILE)])
        step = 256
        for k in range(0, kh, step):
            turns = dot(columns, k_parts[:, half * kh + k : half * kh + k + step], TN)
            for value, to in zip(cos_sin_turns(turns), (k, kh + k)):
                v_high, v_low = split(value)
                high[half, pl.ds(at, TILE), to : to + step] = v_high
                low[half, pl.ds(at, TILE), to : to + step] = v_low

    def gather_sums(half, at, with_density):
        rows = 2 * c + (16 if with_density else 0)
        one = dot(lhs[:rows, pl.ds(at, TILE)], high[half, pl.ds(at, TILE), :], NN)
        two = dot(lhs[:c, pl.ds(at, TILE)], low[half, pl.ds(at, TILE), :], NN)
        sums[half] += one[:c] + one[c : 2 * c] + two
        if with_density:
            three = dot(lhs[2 * c :, pl.ds(at, TILE)], low[half, pl.ds(at, TILE), :], NN)
            density[half] += (one[2 * c :] + three)[:8]

    def first_pass(half):
        def body_at(at):
            if half == 0:
                masked = states[pl.ds(at, TILE), :] * occ_column(at)
                place_lhs(at, masked)
                charge[...] += jnp.broadcast_to(jnp.sum(masked, axis=0, keepdims=True), (8, c))
                lane = at + lax.broadcasted_iota(jnp.int32, (16, TILE), 1)
                lhs[2 * c :, pl.ds(at, TILE)] = (lane < tally[0]).astype(jnp.float32).astype(jnp.bfloat16)
            phases(half, at)
            gather_sums(half, at, True)

        return body_at

    def finish_sums(layer, half):
        for k in range(0, wide, c):
            part[layer, half, k : k + c, :] = sums[half, :, k : k + c].T

    def place_small(layer):
        if layer == 0:
            for half in range(2):
                for i in range(wide // c):
                    small[0, 0, half * (wide // c) + i : half * (wide // c) + i + 1, :] = density[
                        half, :1, i * c : (i + 1) * c
                    ]
        else:
            small[1, 0, : 2 * wide // c, :] = jnp.zeros((2 * wide // c, c), jnp.float32)
        base = 2 * wide // c
        small[layer, 0, base : base + 8, :] = charge[...]
        small[layer, 0, base + 8 : base + 16, :] = jnp.full((8, c), tally[0], jnp.int32).astype(jnp.float32)

    def weigh(layer, half):
        base = 2 * wide // c
        mean = small[layer, bits, base : base + 1, :] / small[layer, bits, base + 8 : base + 9, :]
        root = jnp.sqrt(small[layer, bits, base + 8 : base + 9, :])
        for i in range(wide // c):
            row = half * (wide // c) + i
            dens = jnp.broadcast_to(small[0, bits, row : row + 1, :], (c, c)).T
            k = half * kh + (i * c) % kh
            value = (full[layer, half, i * c : (i + 1) * c, :] - dens * mean) / root
            v_high, v_low = split(value * kernels[layer, k : k + c, :])
            w[half, i * c : (i + 1) * c, :c] = v_high
            w[half, i * c : (i + 1) * c, c:] = v_low

    def potential_at(half, at):
        both = dot(high[half, pl.ds(at, TILE), :], w[half], NN)
        return both[:, :c] + both[:, c:] + dot(low[half, pl.ds(at, TILE), :], w[half, :, :c], NN)

    def updated(layer, source, at):
        value = potential[pl.ds(at, TILE), :] + potential_at(1, at)
        v = times_split(value, first_matrix[layer])
        return source[pl.ds(at, TILE), :] + times_split(v / (1.0 + jnp.exp(-v)), second_matrix[layer])

    def keep_potential(at):
        potential[pl.ds(at, TILE), :] = potential_at(0, at)

    def middle(at):
        value = updated(0, states, at)
        fresh[pl.ds(at, TILE), :] = value
        masked = value * occ_column(at)
        place_lhs(at, masked)
        charge[...] += jnp.broadcast_to(jnp.sum(masked, axis=0, keepdims=True), (8, c))
        gather_sums(0, at, False)

    def last(at):
        out[pl.ds(at, TILE), :] = updated(1, fresh, at) * occ_column(at)

    def during(steps, pieces, body_at):
        step = slots // pieces
        for i in range(pieces):
            run_tiles(i * step, (i + 1) * step, TILE, body_at)
            advance(*steps)

    def drain(*steps):
        while advance(*steps):
            pass

    sums[...] = jnp.zeros_like(sums)
    density[...] = jnp.zeros_like(density)
    charge[...] = jnp.zeros_like(charge)
    for layer in range(2):
        if layer == 0:
            run_tiles(0, slots, TILE, first_pass(0))
        else:
            sums[...] = jnp.zeros_like(sums)
            charge[...] = jnp.zeros_like(charge)
            run_tiles(0, slots, TILE, middle)
        finish_sums(layer, 0)
        a = big(layer, 0)
        advance(a)
        during([a], PIECES, first_pass(1) if layer == 0 else lambda at: gather_sums(1, at, False))
        finish_sums(layer, 1)
        place_small(layer)
        b, x = big(layer, 1), little(layer)
        drain_first(a, b, x)
        weigh(layer, 0)
        during([b], PIECES, keep_potential)
        drain(b)
        weigh(layer, 1)
    run_tiles(0, slots, TILE, last)


def drain_first(a, b, x):
    while True:
        live = [next(one, "end") != "end" for one in (a, x)]
        next(b, "end")
        if not any(live):
            return


def body(states, coords, tallies, lattice, kernels, first_matrix, second_matrix):
    slots, c = states.shape
    kspace = lattice.shape[1]
    bits = lax.axis_size("slab").bit_length() - 1
    f32, b16 = jnp.float32, jnp.bfloat16
    coords8 = jnp.pad(coords, ((0, 5), (0, 0)))
    k8 = jnp.pad(lattice, ((0, 5), (0, 0))).astype(b16)
    k_parts = jnp.concatenate([k8, k8, k8, k8], 0)
    vmem = pl.BlockSpec(memory_space=pltpu.VMEM)
    extra = 2 * kspace // c + 16
    return pl.pallas_call(
        functools.partial(ewald_kernel, bits),
        in_specs=[pl.BlockSpec(memory_space=pltpu.SMEM)] + [vmem] * 6,
        out_specs=vmem,
        out_shape=jax.ShapeDtypeStruct((slots, c), f32),
        scratch_shapes=[
            pltpu.VMEM((2, slots, kspace), b16),
            pltpu.VMEM((2, slots, kspace), b16),
            pltpu.VMEM((2 * c + 16, slots), b16),
            pltpu.VMEM((2, c, kspace), f32),
            pltpu.VMEM((2, 8, kspace), f32),
            pltpu.VMEM((8, c), f32),
            pltpu.VMEM((2, kspace, 2 * c), b16),
            pltpu.VMEM((slots, c), f32),
            pltpu.VMEM((slots, c), f32),
            pltpu.VMEM((2, 2, kspace, c), f32),
            pltpu.VMEM((2, 2, kspace, c), f32),
            pltpu.VMEM((2, 2, kspace, c), f32),
            pltpu.VMEM((2, bits + 1, extra, c), f32),
            pltpu.VMEM((2, bits, extra, c), f32),
            pltpu.SemaphoreType.DMA((2, 2, 2 * bits)),
            pltpu.SemaphoreType.DMA((2, 2, 2 * bits)),
            pltpu.SemaphoreType.DMA((2, bits)),
            pltpu.SemaphoreType.DMA((2, bits)),
        ],
        compiler_params=pltpu.CompilerParams(
            vmem_limit_bytes=62 * 2**20, collective_id=0, has_side_effects=True
        ),
    )(tallies, states, coords8, k_parts, kernels, first_matrix, second_matrix)


def solution(mesh):
    in_specs = (
        P(("groups", "slab"), None),
        P(None, ("groups", "slab")),
        P(("groups", "slab")),
        P(),
        P(),
        P(),
        P(),
    )
    out_specs = P(("groups", "slab"), None)
    return jax.shard_map(body, mesh=mesh, in_specs=in_specs, out_specs=out_specs, check_vma=False)
```
